32 devices in a mesh: row: 4 (over x, core), col: 8 (over z, y).
Axes of the slice: x: 2, y: 2, z: 4, core: 2. Of those that a mesh axis runs over, the one named last changes fastest.
Arguments:
- kernel: float32 [2048, 2048], P('row', 'col'), may hold values from -6 to 6
- margin: float32 [2048, 2048], P('row', 'col'), may hold values from -0.0029296875 to 0.0029296875
- grid_values: bfloat16 [2048, 16384], P(None, 'col'), may hold values from -0.125 to 0.125
- proj_margins: bfloat16 [2048, 4096], P(None, 'col'), may hold values from -0.125 to 0.125
- kernel_pattern: int32 [16, 16], replicated, may hold values 0 or 1
- margin_pattern: int32 [16, 16], replicated, may hold values 0 or 1
- box_pattern: int32 [128, 16], P('col'), may hold values 0 or 1
- proj_pattern: int32 [256, 16], P('col'), may hold values 0 or 1
Outputs:
- kernel_out: float32 [2048, 2048], P('row', 'col')
- occupancy: float32 [256, 256], P('col')
- density: float32 [16384], P('col')
The draws below stay inside these ranges and needn't reach their ends.
All inputs are finite; a program needn't handle non-finite values. No bound on the sum of `box_pattern` or of `proj_pattern` on one device may be relied on, other than what follows from the above.
Results may differ from the reference program's by a relative error of at most 0.0065.
Values may be sent and summed in bfloat16 or wider, within the bound.
A program may use at most 128 MiB of HBM per device.

```python
import jax
import jax.numpy as jnp
from jax import lax

TILE = 128
BOXPTS = 128
NPROJ = 16
NGWF = 2048
NT = 16
NATOM = 256
PJ = 4096
GRID = 16384
NBOX = 128


def place_ends(values, key, smallest, high):
    spot = [jax.random.randint(jax.random.fold_in(key, axis), (), 0, length) for axis, length in enumerate(values.shape)]
    longest = values.shape.index(max(values.shape))
    next_to = spot[:longest] + [(spot[longest] + 1) % values.shape[longest]] + spot[longest + 1:]
    return values.at[tuple(spot)].set(smallest).at[tuple(next_to)].set(high)


def block_levels(own_key, extent, pieces, least, high):
    level, own = 1.0, jax.random.fold_in(own_key, 6)
    for axis_at, blocks in pieces:
        draws = jnp.exp(jax.random.uniform(jax.random.fold_in(own, axis_at), (blocks,), jnp.float32, least / len(pieces), high / len(pieces)))
        level = level * jnp.repeat(draws, extent[axis_at] // blocks).reshape([-1 if axis == axis_at else 1 for axis in range(len(extent))])
    return level


def scatter_about(own_key, shape, width, bound, shards=(), kind=jnp.bfloat16):
    drawn = width * jax.random.normal(own_key, shape, jnp.float32)
    if shards:
        drawn = drawn * block_levels(own_key, shape, shards, -0.22, 0.18)
    return jnp.clip(drawn, -bound, bound).astype(kind)


def setup_inputs(seed: int = 0) -> dict:
    keys = jax.random.split(jax.random.key(seed), 9)
    return {
        "kernel": scatter_about(keys[0], (NGWF, NGWF), 1.0, 6.0, ((0, 4), (1, 8)), jnp.float32),
        "margin": scatter_about(keys[1], (NGWF, NGWF), (NGWF * NGWF) ** -0.5, 0.0029296875, ((0, 4), (1, 8)), jnp.float32),
        "grid_values": scatter_about(keys[2], (NGWF, GRID), NGWF ** -0.5, 0.125, ((1, 8),)),
        "proj_margins": scatter_about(keys[3], (NGWF, PJ), NGWF ** -0.5, 0.125, ((1, 8),)),
        "kernel_pattern": place_ends((jax.random.randint(keys[4], (NT, NT), 0, 3) < 2).astype(jnp.int32), jax.random.fold_in(keys[4], 1), 0, 1),
        "margin_pattern": place_ends((jax.random.randint(keys[5], (NT, NT), 0, 3) < 2).astype(jnp.int32), jax.random.fold_in(keys[5], 1), 0, 1),
        "box_pattern": place_ends((jax.random.randint(keys[6], (NBOX, NT), 0, 3) < 2).astype(jnp.int32), jax.random.fold_in(keys[6], 1), 0, 1),
        "proj_pattern": place_ends((jax.random.randint(keys[7], (NATOM, NT), 0, 3) < 2).astype(jnp.int32), jax.random.fold_in(keys[7], 1), 0, 1),
    }


def expand(pattern, first, second):
    return jnp.repeat(jnp.repeat(pattern, first, 0), second, 1)


def reference(kernel, margin, grid_values, proj_margins, kernel_pattern, margin_pattern, box_pattern, proj_pattern):
    exact = lax.Precision.HIGHEST
    kernel_sparse = kernel * expand(kernel_pattern, TILE, TILE).astype(jnp.float32)
    margin_sparse = margin * expand(margin_pattern, TILE, TILE).astype(jnp.float32)
    ks_product = jnp.dot(kernel_sparse, margin_sparse, precision=exact, preferred_element_type=jnp.float32)
    ksk_product = jnp.dot(ks_product, kernel_sparse, precision=exact, preferred_element_type=jnp.float32)
    quintic = jnp.dot(ks_product, ksk_product, precision=exact, preferred_element_type=jnp.float32)
    kernel_out = 3.0 * ksk_product - 2.0 * quintic
    kernel_half = kernel_out.astype(jnp.bfloat16)
    grid_masked = grid_values * expand(box_pattern.T, TILE, BOXPTS).astype(jnp.bfloat16)
    proj_masked = proj_margins * expand(proj_pattern.T, TILE, NPROJ).astype(jnp.bfloat16)
    grid_image = jnp.dot(kernel_half, grid_masked, preferred_element_type=jnp.float32)
    density = jnp.sum(grid_masked.astype(jnp.float32) * grid_image, axis=0)
    proj_image = jnp.dot(kernel_half, proj_masked, preferred_element_type=jnp.float32)
    left_side = proj_masked.astype(jnp.float32).reshape(NGWF, NATOM, NPROJ)
    right_side = proj_image.reshape(NGWF, NATOM, NPROJ)
    occupancy = jnp.einsum("aki,akj->kij", left_side, right_side).reshape(NATOM, NPROJ * NPROJ)
    return kernel_out, occupancy, density
```

```python
import jax
import jax.numpy as jnp
from jax import lax
from jax.sharding import PartitionSpec as P

TILE = 128
BOXPTS = 128
NPROJ = 16


def expand(pattern, first, second):
    return jnp.repeat(jnp.repeat(pattern, first, 0), second, 1)


def folder(panel, piece):
    return jnp.dot(
        panel, piece, preferred_element_type=jnp.float32
    )


def on_device(
    kernel,
    margin,
    grid_values,
    proj_margins,
    kernel_pattern,
    margin_pattern,
    box_pattern,
    proj_pattern,
):
    row_index = lax.axis_index("row")
    col_index = lax.axis_index("col")
    local_rows = kernel.shape[0]
    local_cols = kernel.shape[1]
    row_tiles = local_rows // TILE
    col_tiles = local_cols // TILE
    starts = (row_index * row_tiles, col_index * col_tiles)
    kernel_block = lax.dynamic_slice(kernel_pattern, starts, (row_tiles, col_tiles))
    margin_block = lax.dynamic_slice(margin_pattern, starts, (row_tiles, col_tiles))
    half = jnp.bfloat16
    kernel_sparse = (kernel * expand(kernel_block, TILE, TILE).astype(jnp.float32)).astype(half)
    margin_sparse = (margin * expand(margin_block, TILE, TILE).astype(jnp.float32)).astype(half)
    kernel_panel = lax.all_gather(kernel_sparse, "col", axis=1, tiled=True)
    ks_product = folder(kernel_panel, lax.all_gather(margin_sparse, "row", axis=0, tiled=True))
    product_panel = lax.all_gather(ks_product.astype(half), "col", axis=1, tiled=True)
    ksk_product = folder(product_panel, lax.all_gather(kernel_sparse, "row", axis=0, tiled=True))
    quintic = folder(product_panel, lax.all_gather(ksk_product.astype(half), "row", axis=0, tiled=True))
    kernel_out = 3.0 * ksk_product - 2.0 * quintic
    kernel_half = kernel_out.astype(jnp.bfloat16)
    half_panel = lax.all_gather(kernel_half, "col", axis=1, tiled=True)
    grid_masked = grid_values * expand(box_pattern.T, TILE, BOXPTS).astype(jnp.bfloat16)
    proj_masked = proj_margins * expand(proj_pattern.T, TILE, NPROJ).astype(jnp.bfloat16)
    first_row = row_index * local_rows
    grid_image = jnp.dot(half_panel, grid_masked, preferred_element_type=jnp.float32)
    grid_local = lax.dynamic_slice_in_dim(grid_masked, first_row, local_rows, 0)
    density_part = jnp.sum(grid_local.astype(jnp.float32) * grid_image, axis=0)
    proj_image = jnp.dot(half_panel, proj_masked, preferred_element_type=jnp.float32)
    proj_local = lax.dynamic_slice_in_dim(proj_masked, first_row, local_rows, 0)
    atoms_local = proj_masked.shape[1] // NPROJ
    left_side = proj_local.astype(jnp.float32).reshape(local_rows, atoms_local, NPROJ)
    right_side = proj_image.reshape(local_rows, atoms_local, NPROJ)
    occupancy_part = jnp.einsum("aki,akj->kij", left_side, right_side).reshape(
        atoms_local, NPROJ * NPROJ
    )
    density, occupancy = lax.psum((density_part, occupancy_part), "row")
    return (kernel_out, occupancy, density)


def solution(mesh):
    in_specs = (
        P("row", "col"),
        P("row", "col"),
        P(None, "col"),
        P(None, "col"),
        P(),
        P(),
        P("col", None),
        P("col", None),
    )
    out_specs = (P("row", "col"), P("col", None), P("col"))
    return jax.shard_map(
        on_device, mesh=mesh, in_specs=in_specs, out_specs=out_specs, check_vma=False
    )
```

```python
import functools

import jax
import jax.numpy as jnp
from jax import lax
from jax.experimental import pallas as pl
from jax.experimental.pallas import tpu as pltpu
from jax.sharding import PartitionSpec as P

TILE = 128
BOXPTS = 128
NPROJ = 16
PIECES = 2
SPAN = 512
F32 = jnp.float32
HALF = jnp.bfloat16
MESH = pl.DeviceIdType.MESH


def spot_at(place, n):
    if n == 8:
        turn = place // 4
        outer = place * (1 - turn) + (7 - place) * turn
        return outer * 2 + turn
    outer, inner = place // 4, place % 4
    odd = outer % 2
    return outer * 4 + inner * (1 - odd) + (3 - inner) * odd


def place_of(spot, n):
    if n == 8:
        outer, turn = spot // 2, spot % 2
        return outer * (1 - turn) + (7 - outer) * turn
    outer, inner = spot // 4, spot % 4
    odd = outer % 2
    return outer * 4 + inner * (1 - odd) + (3 - inner) * odd


def body(
    n_row,
    n_col,
    kernel_ref,
    margin_ref,
    grid_ref,
    proj_ref,
    kpat_ref,
    mpat_ref,
    box_ref,
    ppat_ref,
    out_ref,
    occ_ref,
    dens_ref,
    k_panel,
    m_panel,
    h_panel,
    s_col,
    k_col,
    w_col,
    points,
    mask,
    total,
    image,
    dens_acc,
    pay,
    ring_send,
    ring_recv,
    x_send,
    x_recv,
    core_send,
    core_recv,
    pay_send,
    pay_recv,
    load_sem,
):
    r = lax.axis_index("row")
    c = lax.axis_index("col")
    rows, cols = kernel_ref.shape
    n = rows * n_row
    gcols, pcols = grid_ref.shape[1], proj_ref.shape[1]
    nx = n_row // 2
    x, core = r // 2, r % 2
    place = place_of(c, n_col)

    def spot(k):
        return spot_at(lax.rem(place + k + n_col, n_col), n_col)

    ahead, behind = spot(1), spot(-1)
    others = [lax.rem(r + k, n_row) for k in range(1, n_row)]
    barrier = pltpu.get_barrier_semaphore()
    for other in others:
        pl.semaphore_signal(barrier, inc=1, device_id=(other, c), device_id_type=MESH)
    for other in (ahead, behind):
        pl.semaphore_signal(barrier, inc=1, device_id=(r, other), device_id_type=MESH)

    loads = [
        pltpu.make_async_copy(grid_ref, points.at[:, pl.ds(0, gcols)], load_sem.at[0]),
        pltpu.make_async_copy(proj_ref, points.at[:, pl.ds(gcols, pcols)], load_sem.at[1]),
    ]
    my_rows = pl.ds(pl.multiple_of(r * rows, rows), rows)
    for i in range(rows // TILE):
        for j in range(cols // TILE):
            a, b = pl.ds(i * TILE, TILE), pl.ds(j * TILE, TILE)
            keep = kpat_ref[r * (rows // TILE) + i, c * (cols // TILE) + j].astype(F32)
            block = (kernel_ref[a, b] * keep).astype(HALF)
            k_panel[c, a, b] = block
            k_col[pl.ds(pl.multiple_of(r * rows + i * TILE, TILE), TILE), b] = block
            keep = mpat_ref[r * (rows // TILE) + i, c * (cols // TILE) + j].astype(F32)
            s_col[pl.ds(pl.multiple_of(r * rows + i * TILE, TILE), TILE), b] = (
                margin_ref[a, b] * keep
            ).astype(HALF)

    pl.semaphore_wait(barrier, n_row + 1)
    sent = []

    part = rows // (2 * PIECES)

    def ring_copy(stage, panel, way, piece, step, origin):
        at = panel.at[origin, pl.ds((way * PIECES + piece) * part, part)]
        return pltpu.make_async_remote_copy(
            src_ref=at,
            dst_ref=at,
            send_sem=ring_send.at[stage, way, piece, step],
            recv_sem=ring_recv.at[stage, way, piece, step],
            device_id=(r, ahead if way == 0 else behind),
            device_id_type=MESH,
        )

    def origin_of(way, step):
        return spot(-step if way == 0 else step)

    def ring_start(stage, panel):
        for piece in range(PIECES):
            for way in range(2):
                copy = ring_copy(stage, panel, way, piece, 0, c)
                copy.start()
                sent.append(copy)

    def ring_step(stage, panel, step):
        for piece in range(PIECES):
            for way in range(2):
                origin = origin_of(way, step + 1)
                ring_copy(stage, panel, way, piece, step, origin).wait_recv()
                if step + 1 < n_col - 1:
                    copy = ring_copy(stage, panel, way, piece, step + 1, origin)
                    copy.start()
                    sent.append(copy)

    bit = rows // PIECES

    def x_copy(stage, panel, step, piece, origin):
        at = panel.at[pl.ds(pl.multiple_of(origin * rows + piece * bit, bit), bit)]
        return pltpu.make_async_remote_copy(
            src_ref=at,
            dst_ref=at,
            send_sem=x_send.at[stage, step, piece],
            recv_sem=x_recv.at[stage, step, piece],
            device_id=(lax.rem(x + 1, nx) * 2 + core, c),
            device_id_type=MESH,
        )

    def core_copy(stage, panel, step, piece, origin):
        at = panel.at[pl.ds(pl.multiple_of(origin * rows + piece * bit, bit), bit)]
        return pltpu.make_async_remote_copy(
            src_ref=at,
            dst_ref=at,
            send_sem=core_send.at[stage, step, piece],
            recv_sem=core_recv.at[stage, step, piece],
            device_id=(x * 2 + 1 - core, c),
            device_id_type=MESH,
        )

    def x_origin(step, side):
        return lax.rem(x - step + nx, nx) * 2 + side

    def row_start(stage, panel):
        for piece in range(PIECES):
            for make in (x_copy, core_copy):
                copy = make(stage, panel, 0, piece, r)
                copy.start()
                sent.append(copy)

    def row_relay(stage, panel, step):
        for piece in range(PIECES):
            origin = x_origin(step + 1, core)
            x_copy(stage, panel, step, piece, origin).wait_recv()
            onward = [core_copy(stage, panel, step + 1, piece, origin)]
            if step + 1 < nx - 1:
                onward.append(x_copy(stage, panel, step + 1, piece, origin))
            for copy in onward:
                copy.start()
                sent.append(copy)

    def row_wait(stage, panel, step):
        for piece in range(PIECES):
            core_copy(stage, panel, step, piece, x_origin(step, 1 - core)).wait_recv()

    def row_finish(stage, panel):
        for step in range(nx):
            row_wait(stage, panel, step)

    way_rows = rows // 2

    def multiply(panel, right, way, origin):
        half = pl.ds(way * way_rows, way_rows)
        deep = pl.ds(pl.multiple_of(origin * cols, cols), cols)
        total[half, :] += jnp.dot(
            panel[origin, half, :], right[deep, :], preferred_element_type=F32
        )

    def take(panel, right, step):
        for way in range(2):
            multiply(panel, right, way, origin_of(way, step))

    ring_start(0, k_panel)
    row_start(0, s_col)
    row_start(1, k_col)
    for load in loads:
        load.start()
    for ref, width, first in ((box_ref, BOXPTS, 0), (ppat_ref, NPROJ, gcols)):
        count = ref.shape[0]
        size = count * width
        spread = (
            lax.broadcasted_iota(jnp.int32, (count, size), 1) // width
            == lax.broadcasted_iota(jnp.int32, (count, size), 0)
        ).astype(F32)
        mask[:, pl.ds(first, size)] = lax.dot_general(
            ref[...].astype(F32), spread, (((0,), (0,)), ((), ())), preferred_element_type=F32
        )

    n_tiles = n // TILE

    def mask_tile(tile, _):
        at = pl.ds(pl.multiple_of(tile * TILE, TILE), TILE)
        keep = mask[pl.ds(tile, 1), :].astype(HALF)
        points[at, :] = points[at, :] * keep
        return 0

    total[...] = jnp.zeros_like(total)
    dens_acc[...] = jnp.zeros_like(dens_acc)
    image[...] = jnp.zeros_like(image)
    pay[...] = jnp.zeros_like(pay)
    for step in range(n_col - 1):
        ring_step(0, k_panel, step)
        if step == 2:
            for k in range(nx - 1):
                row_relay(0, s_col, k)
        if step == 4:
            row_finish(0, s_col)
            for k in range(step + 1):
                take(k_panel, s_col, k)
        if step > 4:
            take(k_panel, s_col, step)
        if step == 5:
            for k in range(nx - 1):
                row_relay(1, k_col, k)
    take(k_panel, s_col, n_col - 1)

    m_panel[c] = total[...].astype(HALF)
    ring_start(1, m_panel)
    row_finish(1, k_col)
    total[...] = jnp.zeros_like(total)
    take(m_panel, k_col, 0)
    for load in loads:
        load.wait()
    per = (n_tiles + n_col - 3) // (n_col - 2)
    for step in range(n_col - 1):
        ring_step(1, m_panel, step)
        take(m_panel, k_col, step + 1)
        if step < n_col - 2:
            lax.fori_loop(
                min(step * per, n_tiles), min((step + 1) * per, n_tiles), mask_tile, 0
            )

    w_col[my_rows, :] = total[...].astype(HALF)
    row_start(2, w_col)
    out_ref[...] = 3.0 * total[...]
    total[...] = jnp.zeros_like(total)
    span = rows // cols

    def quintic(origin):
        for k in range(span):
            for way in range(2):
                multiply(m_panel, w_col, way, origin * span + k)

    quintic(r)
    row_wait(2, w_col, 0)
    quintic(x * 2 + 1 - core)
    for step in range(nx - 1):
        row_relay(2, w_col, step)
        quintic(x_origin(step + 1, core))
        row_wait(2, w_col, step + 1)
        quintic(x_origin(step + 1, 1 - core))

    result = out_ref[...] - 2.0 * total[...]
    out_ref[...] = result
    h_panel[c] = result.astype(HALF)
    ring_start(2, h_panel)

    def apply(step):
        for way in range(2):
            origin = origin_of(way, step)
            half = pl.ds(way * way_rows, way_rows)
            deep = pl.ds(pl.multiple_of(origin * cols, cols), cols)
            local = pl.ds(pl.multiple_of(r * rows + way * way_rows, way_rows), way_rows)

            def tile(t, _):
                at = pl.ds(pl.multiple_of(t * SPAN, SPAN), SPAN)
                made = jnp.dot(
                    h_panel[origin, half, :], points[deep, at], preferred_element_type=F32
                )
                made = made * points[local, at].astype(F32)
                dens_acc[:, at] += jnp.sum(made.reshape(way_rows // 8, 8, SPAN), axis=0)
                return 0

            lax.fori_loop(0, gcols // SPAN, tile, 0)
            image[half, :] += jnp.dot(
                h_panel[origin, half, :],
                points[deep, pl.ds(gcols, pcols)],
                preferred_element_type=F32,
            )

    apply(0)
    for step in range(n_col - 1):
        ring_step(2, h_panel, step)
        apply(step + 1)

    for t in range(gcols // SPAN):
        pay[r, pl.ds(NPROJ + t, 1), :] = jnp.sum(
            dens_acc[:, pl.ds(t * SPAN, SPAN)], axis=0, keepdims=True
        )
    same = (
        lax.broadcasted_iota(jnp.int32, (TILE, TILE), 0) // NPROJ
        == lax.broadcasted_iota(jnp.int32, (TILE, TILE), 1) // NPROJ
    )
    for b in range(pcols // TILE):
        at = pl.ds(b * TILE, TILE)
        left = points[my_rows, pl.ds(gcols + b * TILE, TILE)]
        whole = image[:, at]
        high = whole.astype(HALF)
        low = (whole - high.astype(F32)).astype(HALF)
        dims = (((0,), (0,)), ((), ()))
        full = lax.dot_general(left, high, dims, preferred_element_type=F32)
        full += lax.dot_general(left, low, dims, preferred_element_type=F32)
        full = jnp.where(same, full, 0.0)
        pay[r, pl.ds(0, NPROJ), at] = jnp.sum(
            full.reshape(TILE // NPROJ, NPROJ, TILE), axis=0
        )

    def pay_copy(k, origin):
        return pltpu.make_async_remote_copy(
            src_ref=pay.at[origin],
            dst_ref=pay.at[origin],
            send_sem=pay_send.at[k],
            recv_sem=pay_recv.at[k],
            device_id=(others[k], c),
            device_id_type=MESH,
        )

    for k in range(n_row - 1):
        copy = pay_copy(k, r)
        copy.start()
        sent.append(copy)
    for k in range(n_row - 1):
        pay_copy(k, lax.rem(r - k - 1 + n_row, n_row)).wait_recv()
    gathered = pay[0]
    for k in range(1, n_row):
        gathered = gathered + pay[k]
    occ_ref[...] = gathered[:NPROJ]
    dens_ref[...] = gathered[NPROJ : NPROJ + gcols // SPAN]
    for copy in sent:
        copy.wait_send()


def on_device(
    n_row,
    n_col,
    kernel,
    margin,
    grid_values,
    proj_margins,
    kernel_pattern,
    margin_pattern,
    box_pattern,
    proj_pattern,
):
    rows, cols = kernel.shape
    n = rows * n_row
    gcols, pcols = grid_values.shape[1], proj_margins.shape[1]
    nx = n_row // 2
    dma = pltpu.SemaphoreType.DMA
    vmem = pl.BlockSpec(memory_space=pltpu.VMEM)
    smem = pl.BlockSpec(memory_space=pltpu.SMEM)
    far = pl.BlockSpec(memory_space=pl.ANY)
    out, occ, dens = pl.pallas_call(
        functools.partial(body, n_row, n_col),
        out_shape=(
            jax.ShapeDtypeStruct((rows, cols), F32),
            jax.ShapeDtypeStruct((NPROJ, pcols), F32),
            jax.ShapeDtypeStruct((gcols // SPAN, SPAN), F32),
        ),
        in_specs=[vmem, vmem, far, far, smem, smem, vmem, vmem],
        out_specs=(vmem, vmem, vmem),
        scratch_shapes=[
            pltpu.VMEM((n_col, rows, cols), HALF),
            pltpu.VMEM((n_col, rows, cols), HALF),
            pltpu.VMEM((n_col, rows, cols), HALF),
            pltpu.VMEM((n, cols), HALF),
            pltpu.VMEM((n, cols), HALF),
            pltpu.VMEM((n, cols), HALF),
            pltpu.VMEM((n, gcols + pcols), HALF),
            pltpu.VMEM((n // TILE, gcols + pcols), F32),
            pltpu.VMEM((rows, cols), F32),
            pltpu.VMEM((rows, pcols), F32),
            pltpu.VMEM((8, gcols), F32),
            pltpu.VMEM((n_row, NPROJ + 8, SPAN), F32),
            dma((3, 2, PIECES, n_col - 1)),
            dma((3, 2, PIECES, n_col - 1)),
            dma((3, nx - 1, PIECES)),
            dma((3, nx - 1, PIECES)),
            dma((3, nx, PIECES)),
            dma((3, nx, PIECES)),
            dma((n_row - 1,)),
            dma((n_row - 1,)),
            dma((2,)),
        ],
        compiler_params=pltpu.CompilerParams(
            collective_id=0, has_side_effects=True, vmem_limit_bytes=58 * 1024 * 1024
        ),
    )(
        kernel,
        margin,
        grid_values,
        proj_margins,
        kernel_pattern,
        margin_pattern,
        box_pattern,
        proj_pattern,
    )
    atoms = pcols // NPROJ
    occupancy = occ.reshape(NPROJ, atoms, NPROJ).transpose(1, 0, 2).reshape(atoms, NPROJ * NPROJ)
    return (out, occupancy, dens.reshape(gcols))


def solution(mesh):
    in_specs = (
        P("row", "col"),
        P("row", "col"),
        P(None, "col"),
        P(None, "col"),
        P(),
        P(),
        P("col", None),
        P("col", None),
    )
    out_specs = (P("row", "col"), P("col", None), P("col"))
    return jax.shard_map(
        functools.partial(on_device, mesh.shape["row"], mesh.shape["col"]),
        mesh=mesh,
        in_specs=in_specs,
        out_specs=out_specs,
        check_vma=False,
    )
```

```python
import functools

import jax
import jax.numpy as jnp
from jax import lax
from jax.experimental import pallas as pl
from jax.experimental.pallas import tpu as pltpu
from jax.sharding import PartitionSpec as P

TILE = 128
BOXPTS = 128
NPROJ = 16
PIECES = 4
SPAN = 512
F32 = jnp.float32
HALF = jnp.bfloat16
MESH = pl.DeviceIdType.MESH


def spot_at(place, n):
    if n == 8:
        turn = place // 4
        outer = place * (1 - turn) + (7 - place) * turn
        return outer * 2 + turn
    outer, inner = place // 4, place % 4
    odd = outer % 2
    return outer * 4 + inner * (1 - odd) + (3 - inner) * odd


def place_of(spot, n):
    if n == 8:
        outer, turn = spot // 2, spot % 2
        return outer * (1 - turn) + (7 - outer) * turn
    outer, inner = spot // 4, spot % 4
    odd = outer % 2
    return outer * 4 + inner * (1 - odd) + (3 - inner) * odd


def body(
    n_row,
    n_col,
    kernel_ref,
    margin_ref,
    grid_ref,
    proj_ref,
    kpat_ref,
    mpat_ref,
    box_ref,
    ppat_ref,
    out_ref,
    occ_ref,
    dens_ref,
    k_panel,
    m_panel,
    h_panel,
    s_col,
    k_col,
    w_col,
    points,
    mask,
    total,
    image,
    dens_acc,
    pay,
    ring_send,
    ring_recv,
    x_send,
    x_recv,
    core_send,
    core_recv,
    pay_send,
    pay_recv,
    load_sem,
):
    r = lax.axis_index("row")
    c = lax.axis_index("col")
    rows, cols = kernel_ref.shape
    n = rows * n_row
    gcols, pcols = grid_ref.shape[1], proj_ref.shape[1]
    nx = n_row // 2
    x, core = r // 2, r % 2
    place = place_of(c, n_col)

    def spot(k):
        return spot_at(lax.rem(place + k + n_col, n_col), n_col)

    ahead, behind = spot(1), spot(-1)
    others = [lax.rem(r + k, n_row) for k in range(1, n_row)]
    barrier = pltpu.get_barrier_semaphore()
    for other in others:
        pl.semaphore_signal(barrier, inc=1, device_id=(other, c), device_id_type=MESH)
    for other in (ahead, behind):
        pl.semaphore_signal(barrier, inc=1, device_id=(r, other), device_id_type=MESH)

    loads = [
        pltpu.make_async_copy(grid_ref, points.at[:, pl.ds(0, gcols)], load_sem.at[0]),
        pltpu.make_async_copy(proj_ref, points.at[:, pl.ds(gcols, pcols)], load_sem.at[1]),
    ]
    my_rows = pl.ds(pl.multiple_of(r * rows, rows), rows)
    for i in range(rows // TILE):
        for j in range(cols // TILE):
            a, b = pl.ds(i * TILE, TILE), pl.ds(j * TILE, TILE)
            keep = kpat_ref[r * (rows // TILE) + i, c * (cols // TILE) + j].astype(F32)
            block = (kernel_ref[a, b] * keep).astype(HALF)
            k_panel[c, a, b] = block
            k_col[pl.ds(pl.multiple_of(r * rows + i * TILE, TILE), TILE), b] = block
            keep = mpat_ref[r * (rows // TILE) + i, c * (cols // TILE) + j].astype(F32)
            s_col[pl.ds(pl.multiple_of(r * rows + i * TILE, TILE), TILE), b] = (
                margin_ref[a, b] * keep
            ).astype(HALF)

    pl.semaphore_wait(barrier, n_row + 1)
    sent = []

    part = rows // (2 * PIECES)

    def ring_copy(stage, panel, way, piece, step, origin):
        at = panel.at[origin, pl.ds((way * PIECES + piece) * part, part)]
        return pltpu.make_async_remote_copy(
            src_ref=at,
            dst_ref=at,
            send_sem=ring_send.at[stage, way, piece, step],
            recv_sem=ring_recv.at[stage, way, piece, step],
            device_id=(r, ahead if way == 0 else behind),
            device_id_type=MESH,
        )

    def origin_of(way, step):
        return spot(-step if way == 0 else step)

    def ring_start(stage, panel):
        for piece in range(PIECES):
            for way in range(2):
                copy = ring_copy(stage, panel, way, piece, 0, c)
                copy.start()
                sent.append(copy)

    def ring_step(stage, panel, step):
        for piece in range(PIECES):
            for way in range(2):
                origin = origin_of(way, step + 1)
                ring_copy(stage, panel, way, piece, step, origin).wait_recv()
                if step + 1 < n_col - 1:
                    copy = ring_copy(stage, panel, way, piece, step + 1, origin)
                    copy.start()
                    sent.append(copy)

    bit = rows // PIECES

    def x_copy(stage, panel, step, piece, origin):
        at = panel.at[pl.ds(pl.multiple_of(origin * rows + piece * bit, bit), bit)]
        return pltpu.make_async_remote_copy(
            src_ref=at,
            dst_ref=at,
            send_sem=x_send.at[stage, step, piece],
            recv_sem=x_recv.at[stage, step, piece],
            device_id=(lax.rem(x + 1, nx) * 2 + core, c),
            device_id_type=MESH,
        )

    def core_copy(stage, panel, step, piece, origin):
        at = panel.at[pl.ds(pl.multiple_of(origin * rows + piece * bit, bit), bit)]
        return pltpu.make_async_remote_copy(
            src_ref=at,
            dst_ref=at,
            send_sem=core_send.at[stage, step, piece],
            recv_sem=core_recv.at[stage, step, piece],
            device_id=(x * 2 + 1 - core, c),
            device_id_type=MESH,
        )

    def x_origin(step, side):
        return lax.rem(x - step + nx, nx) * 2 + side

    def row_start(stage, panel):
        for piece in range(PIECES):
            for make in (x_copy, core_copy):
                copy = make(stage, panel, 0, piece, r)
                copy.start()
                sent.append(copy)

    def row_relay(stage, panel, step):
        for piece in range(PIECES):
            origin = x_origin(step + 1, core)
            x_copy(stage, panel, step, piece, origin).wait_recv()
            onward = [core_copy(stage, panel, step + 1, piece, origin)]
            if step + 1 < nx - 1:
                onward.append(x_copy(stage, panel, step + 1, piece, origin))
            for copy in onward:
                copy.start()
                sent.append(copy)

    def row_wait(stage, panel, step):
        for piece in range(PIECES):
            core_copy(stage, panel, step, piece, x_origin(step, 1 - core)).wait_recv()

    def row_finish(stage, panel):
        for step in range(nx):
            row_wait(stage, panel, step)

    way_rows = rows // 2

    def multiply(panel, right, way, origin):
        half = pl.ds(way * way_rows, way_rows)
        deep = pl.ds(pl.multiple_of(origin * cols, cols), cols)
        total[half, :] += jnp.dot(
            panel[origin, half, :], right[deep, :], preferred_element_type=F32
        )

    def take(panel, right, step):
        for way in range(2):
            multiply(panel, right, way, origin_of(way, step))

    ring_start(0, k_panel)
    row_start(0, s_col)
    row_start(1, k_col)
    for load in loads:
        load.start()
    for ref, width, first, axis in ((box_ref, BOXPTS, 0, 0), (ppat_ref, NPROJ, gcols, 1)):
        count = ref.shape[axis]
        size = count * width
        spread = (
            lax.broadcasted_iota(jnp.int32, (count, size), 1) // width
            == lax.broadcasted_iota(jnp.int32, (count, size), 0)
        ).astype(F32)
        mask[:, pl.ds(first, size)] = lax.dot_general(
            ref[...].astype(F32), spread, (((axis,), (0,)), ((), ())), preferred_element_type=F32
        )

    n_tiles = n // TILE

    def mask_tile(tile, _):
        at = pl.ds(pl.multiple_of(tile * TILE, TILE), TILE)
        keep = mask[pl.ds(tile, 1), :].astype(HALF)
        points[at, :] = points[at, :] * keep
        return 0

    total[...] = jnp.zeros_like(total)
    dens_acc[...] = jnp.zeros_like(dens_acc)
    image[...] = jnp.zeros_like(image)
    pay[...] = jnp.zeros_like(pay)
    for step in range(n_col - 1):
        ring_step(0, k_panel, step)
        if step == 2:
            for k in range(nx - 1):
                row_relay(0, s_col, k)
        if step == 4:
            row_finish(0, s_col)
            for k in range(step + 1):
                take(k_panel, s_col, k)
        if step > 4:
            take(k_panel, s_col, step)
        if step == 5:
            for k in range(nx - 1):
                row_relay(1, k_col, k)
    take(k_panel, s_col, n_col - 1)

    m_panel[c] = total[...].astype(HALF)
    ring_start(1, m_panel)
    row_finish(1, k_col)
    total[...] = jnp.zeros_like(total)
    take(m_panel, k_col, 0)
    for load in loads:
        load.wait()
    per = (n_tiles + n_col - 3) // (n_col - 2)
    for step in range(n_col - 1):
        ring_step(1, m_panel, step)
        take(m_panel, k_col, step + 1)
        if step < n_col - 2:
            lax.fori_loop(
                min(step * per, n_tiles), min((step + 1) * per, n_tiles), mask_tile, 0
            )

    w_col[my_rows, :] = total[...].astype(HALF)
    row_start(2, w_col)
    out_ref[...] = 3.0 * total[...]
    total[...] = jnp.zeros_like(total)
    span = rows // cols

    def quintic(origin):
        for k in range(span):
            for way in range(2):
                multiply(m_panel, w_col, way, origin * span + k)

    quintic(r)
    row_wait(2, w_col, 0)
    quintic(x * 2 + 1 - core)
    for step in range(nx - 1):
        row_relay(2, w_col, step)
        quintic(x_origin(step + 1, core))
        row_wait(2, w_col, step + 1)
        quintic(x_origin(step + 1, 1 - core))

    result = out_ref[...] - 2.0 * total[...]
    out_ref[...] = result
    h_panel[c] = result.astype(HALF)
    ring_start(2, h_panel)

    def apply(step):
        for way in range(2):
            origin = origin_of(way, step)
            half = pl.ds(way * way_rows, way_rows)
            deep = pl.ds(pl.multiple_of(origin * cols, cols), cols)
            local = pl.ds(pl.multiple_of(r * rows + way * way_rows, way_rows), way_rows)

            def tile(t, _):
                at = pl.ds(pl.multiple_of(t * SPAN, SPAN), SPAN)
                made = jnp.dot(
                    h_panel[origin, half, :], points[deep, at], preferred_element_type=F32
                )
                made = made * points[local, at].astype(F32)
                dens_acc[:, at] += jnp.sum(made.reshape(way_rows // 8, 8, SPAN), axis=0)
                return 0

            lax.fori_loop(0, gcols // SPAN, tile, 0)
            image[half, :] += jnp.dot(
                h_panel[origin, half, :],
                points[deep, pl.ds(gcols, pcols)],
                preferred_element_type=F32,
            )

    apply(0)
    for step in range(n_col - 1):
        ring_step(2, h_panel, step)
        apply(step + 1)

    for t in range(gcols // SPAN):
        pay[r, pl.ds(NPROJ + t, 1), :] = jnp.sum(
            dens_acc[:, pl.ds(t * SPAN, SPAN)], axis=0, keepdims=True
        )
    same = (
        lax.broadcasted_iota(jnp.int32, (TILE, TILE), 0) // NPROJ
        == lax.broadcasted_iota(jnp.int32, (TILE, TILE), 1) // NPROJ
    )
    for b in range(pcols // TILE):
        at = pl.ds(b * TILE, TILE)
        left = points[my_rows, pl.ds(gcols + b * TILE, TILE)]
        whole = image[:, at]
        high = whole.astype(HALF)
        low = (whole - high.astype(F32)).astype(HALF)
        dims = (((0,), (0,)), ((), ()))
        full = lax.dot_general(left, high, dims, preferred_element_type=F32)
        full += lax.dot_general(left, low, dims, preferred_element_type=F32)
        full = jnp.where(same, full, 0.0)
        pay[r, pl.ds(0, NPROJ), at] = jnp.sum(
            full.reshape(TILE // NPROJ, NPROJ, TILE), axis=0
        )

    def pay_copy(k, origin):
        return pltpu.make_async_remote_copy(
            src_ref=pay.at[origin],
            dst_ref=pay.at[origin],
            send_sem=pay_send.at[k],
            recv_sem=pay_recv.at[k],
            device_id=(others[k], c),
            device_id_type=MESH,
        )

    for k in range(n_row - 1):
        copy = pay_copy(k, r)
        copy.start()
        sent.append(copy)
    for k in range(n_row - 1):
        pay_copy(k, lax.rem(r - k - 1 + n_row, n_row)).wait_recv()
    gathered = pay[0]
    for k in range(1, n_row):
        gathered = gathered + pay[k]
    occ_ref[...] = gathered[:NPROJ]
    dens_ref[...] = gathered[NPROJ : NPROJ + gcols // SPAN]
    for copy in sent:
        copy.wait_send()


def on_device(
    n_row,
    n_col,
    kernel,
    margin,
    grid_values,
    proj_margins,
    kernel_pattern,
    margin_pattern,
    box_pattern,
    proj_pattern,
):
    rows, cols = kernel.shape
    n = rows * n_row
    gcols, pcols = grid_values.shape[1], proj_margins.shape[1]
    nx = n_row // 2
    dma = pltpu.SemaphoreType.DMA
    vmem = pl.BlockSpec(memory_space=pltpu.VMEM)
    smem = pl.BlockSpec(memory_space=pltpu.SMEM)
    far = pl.BlockSpec(memory_space=pl.ANY)
    out, occ, dens = pl.pallas_call(
        functools.partial(body, n_row, n_col),
        out_shape=(
            jax.ShapeDtypeStruct((rows, cols), F32),
            jax.ShapeDtypeStruct((NPROJ, pcols), F32),
            jax.ShapeDtypeStruct((gcols // SPAN, SPAN), F32),
        ),
        in_specs=[vmem, vmem, far, far, smem, smem, vmem, vmem],
        out_specs=(vmem, vmem, vmem),
        scratch_shapes=[
            pltpu.VMEM((n_col, rows, cols), HALF),
            pltpu.VMEM((n_col, rows, cols), HALF),
            pltpu.VMEM((n_col, rows, cols), HALF),
            pltpu.VMEM((n, cols), HALF),
            pltpu.VMEM((n, cols), HALF),
            pltpu.VMEM((n, cols), HALF),
            pltpu.VMEM((n, gcols + pcols), HALF),
            pltpu.VMEM((n // TILE, gcols + pcols), F32),
            pltpu.VMEM((rows, cols), F32),
            pltpu.VMEM((rows, pcols), F32),
            pltpu.VMEM((8, gcols), F32),
            pltpu.VMEM((n_row, NPROJ + 8, SPAN), F32),
            dma((3, 2, PIECES, n_col - 1)),
            dma((3, 2, PIECES, n_col - 1)),
            dma((3, nx - 1, PIECES)),
            dma((3, nx - 1, PIECES)),
            dma((3, nx, PIECES)),
            dma((3, nx, PIECES)),
            dma((n_row - 1,)),
            dma((n_row - 1,)),
            dma((2,)),
        ],
        compiler_params=pltpu.CompilerParams(
            collective_id=0, has_side_effects=True, vmem_limit_bytes=58 * 1024 * 1024
        ),
    )(
        kernel,
        margin,
        grid_values,
        proj_margins,
        kernel_pattern,
        margin_pattern,
        box_pattern,
        proj_pattern.T,
    )
    atoms = pcols // NPROJ
    occupancy = occ.reshape(NPROJ, atoms, NPROJ).transpose(1, 0, 2).reshape(atoms, NPROJ * NPROJ)
    return (out, occupancy, dens.reshape(gcols))


def solution(mesh):
    in_specs = (
        P("row", "col"),
        P("row", "col"),
        P(None, "col"),
        P(None, "col"),
        P(),
        P(),
        P("col", None),
        P("col", None),
    )
    out_specs = (P("row", "col"), P("col", None), P("col"))
    return jax.shard_map(
        functools.partial(on_device, mesh.shape["row"], mesh.shape["col"]),
        mesh=mesh,
        in_specs=in_specs,
        out_specs=out_specs,
        check_vma=False,
    )
```
